1024 devices in a mesh: dp: 16 (over x, core), expert: 64 (over z, y).
Axes of the slice: x: 8, y: 8, z: 8, core: 2. Of those that a mesh axis runs over, the one named last changes fastest.
Arguments:
- tokens: bfloat16 [2048, 7168], P('dp', 'expert'), may hold values from -6 to 6
- routes: int32 [2048, 4], P('dp'), may hold values from 0 to 127, all different within a row; in each aligned block of 128 rows (0 to 127, 128 to 255, ...) at most 12 rows name the same one
- scores: int32 [2048, 4], P('dp'), may hold values from 1 to 16
- down_proj: bfloat16 [7168, 1024], P('expert'), may hold values from -0.0625 to 0.0625
- up_proj: bfloat16 [1024, 7168], P(None, 'expert'), may hold values from -0.1875 to 0.1875
- expert_gate: bfloat16 [1024, 262144], P(None, ('dp', 'expert')), may hold values from -0.1875 to 0.1875
- expert_up: bfloat16 [1024, 262144], P(None, ('dp', 'expert')), may hold values from -0.1875 to 0.1875
- expert_down: bfloat16 [262144, 1024], P(('dp', 'expert')), may hold values from -0.125 to 0.125
- cotangent: bfloat16 [2048, 7168], P('dp', 'expert'), may hold values from -12 to 12
Outputs:
- layer_out: bfloat16 [2048, 7168], P('dp', 'expert')
- token_grad: bfloat16 [2048, 7168], P('dp', 'expert')
- down_grad: float32 [7168, 1024], P('expert', 'dp')
- up_grad: float32 [1024, 7168], P('dp', 'expert')
- expert_gate_grad: bfloat16 [1024, 262144], P(None, ('dp', 'expert'))
- expert_up_grad: bfloat16 [1024, 262144], P(None, ('dp', 'expert'))
- expert_down_grad: bfloat16 [262144, 1024], P(('dp', 'expert'))
The draws below stay inside these ranges and needn't reach their ends.
Inputs may be any that keep to these rules, and one draw needn't show every extreme that they name: `routes`: each row names 4 different experts. Within the 128 tokens of one index of dp no expert is named by more than 12 rows, a bound that some block reaches.
All inputs are finite; a program needn't handle non-finite values.
Results may differ from the reference program's by a relative error of at most 0.025.
Values may be sent and summed in bfloat16 or wider, within the bound.
A program may use at most 32 MiB of HBM per device.

```python
import math
import jax
import jax.numpy as jnp
import numpy as np
from jax import lax

D = 7168
LATENT = 1024
FF = 2048
TOP = 4
EXPERTS = 128
TOK_ROW = 128
TOKENS = 2048
CAP = 12
N_DP = 16


def touch_ends(result, key, low, top_value):
    longest = result.shape.index(max(result.shape))
    spots = []
    for shift in (0, 1):
        where = [jax.random.randint(jax.random.fold_in(key, axis), (), 0, length) for axis, length in enumerate(result.shape)]
        where[longest] = (where[longest] + shift) % result.shape[longest]
        spots.append(tuple(where))
    return result.at[spots[0]].set(low).at[spots[1]].set(top_value)


def block_scale(key, dims, cuts, low, high):
    def one(dim, blocks):
        heights = jax.random.uniform(jax.random.fold_in(jax.random.fold_in(key, 6), dim), (blocks,), jnp.float32, low / len(cuts), high / len(cuts))
        return jnp.repeat(jnp.exp(heights), dims[dim] // blocks).reshape((-1,) + (1,) * (len(dims) - dim - 1))

    gain = one(*cuts[0])
    for cut in cuts[1:]:
        gain = gain * one(*cut)
    return gain


def deal_out(key, own, number, rows, number_of, top, reach, skew):
    sequence = jax.random.permutation(key, number_of)
    heavy_load, common = load_shares(number_of, rows * top, reach, skew, True), load_shares(number_of, rows * top, reach, skew, False)
    places = jnp.arange(number_of)

    def named(tallies, turn):
        used = int((tallies > 0).sum())
        fixed = max(1, used // 4)
        passed = fixed + (places - fixed + turn * (used - fixed)) % max(1, number_of - fixed)
        return jnp.zeros((number_of,), jnp.int32).at[sequence[jnp.where(places < fixed, places, passed)]].set(jnp.asarray(tallies, jnp.int32))

    tallies = jnp.where(number % 4 == 0, named(heavy_load, number // 4), named(common, number - number // 4 - 1))
    mixed = jax.random.permutation(jax.random.fold_in(own, 3), number_of)
    source_of, taker = mixed[0:number_of // 2 * 2:2], mixed[1:number_of // 2 * 2:2]
    slack = jnp.minimum(tallies[source_of] - 1, reach - tallies[taker]) // 2
    slack = jnp.where((source_of == sequence[0]) | (taker == sequence[0]) | (tallies[taker] == 0), 0, jnp.maximum(slack, 0))
    passed = jax.random.randint(jax.random.fold_in(own, 4), (number_of // 2,), 0, 1 << 20) % (slack + 1)
    tallies = tallies.at[source_of].add(-passed).at[taker].add(passed)
    labels = jnp.searchsorted(jnp.cumsum(tallies), jnp.arange(rows * top), side="right").astype(jnp.int32)
    grid = labels.reshape(top, rows).T
    grid = grid[jax.random.permutation(jax.random.fold_in(own, 1), rows)]
    turn = jax.random.randint(jax.random.fold_in(own, 2), (rows, 1), 0, top)
    return jnp.take_along_axis(grid, (jnp.arange(top)[None, :] + turn) % top, axis=1)


def load_shares(number_of, total, limit, lean, full):
    weights = [(1 << 20) // math.isqrt(rank ** lean) + 1 for rank in range(1, number_of + 1)]
    largest = limit if full else min(limit, max(-(-total // number_of), total * weights[0] // sum(weights)))
    least = 1 if total - largest >= number_of - 1 else 0
    given, spare = [largest] + [least] * (number_of - 1), total - largest - least * (number_of - 1)
    while spare > 0:
        free = [i for i in range(1, number_of) if given[i] < largest] or [i for i in range(1, number_of) if given[i] < limit]
        pool, remaining = sum([weights[i] for i in free]), spare
        for i in free:
            extra = min(limit - given[i], max(1, remaining * weights[i] // pool), spare)
            given[i] = given[i] + extra
            spare = spare - extra
    return np.array(given)


def gaussian(rng, dims, scale, limit, pieces=(), kind=jnp.bfloat16):
    result = jax.random.normal(rng, dims, jnp.float32) * scale
    if len(pieces) > 0:
        result = block_scale(rng, dims, pieces, -0.22, 0.18) * result
    return jnp.clip(result, min=-limit, max=limit).astype(kind)


def setup_inputs(seed: int = 0) -> dict:
    arg_keys = jax.random.split(jax.random.key(seed), 10)
    tokens = gaussian(arg_keys[0], (TOKENS, D), 1.0, 6.0, ((0, 16), (1, 64)))
    routes_keys = jax.random.split(jax.random.fold_in(arg_keys[1], 1), TOKENS // TOK_ROW)
    routes_turns = jax.random.permutation(jax.random.fold_in(arg_keys[1], 3), TOKENS // TOK_ROW)
    routes = jax.vmap(lambda own, number: deal_out(jax.random.fold_in(arg_keys[1], 2), own, number, TOK_ROW, EXPERTS, TOP, CAP, 2))(routes_keys, routes_turns).reshape((TOKENS, TOP))
    scores = touch_ends(jax.random.randint(arg_keys[2], (TOKENS, TOP), 1, 17), jax.random.fold_in(arg_keys[2], 1), 1, 16).astype(jnp.int32)
    down_proj = gaussian(arg_keys[3], (D, LATENT), D ** -0.5, 0.0625, ((0, 64),))
    up_proj = gaussian(arg_keys[4], (LATENT, D), LATENT ** -0.5, 0.1875, ((1, 64),))
    expert_gate = gaussian(arg_keys[5], (LATENT, EXPERTS * FF), LATENT ** -0.5, 0.1875, ((1, 1024),))
    expert_up = gaussian(arg_keys[6], (LATENT, EXPERTS * FF), LATENT ** -0.5, 0.1875, ((1, 1024),))
    expert_down = gaussian(arg_keys[7], (EXPERTS * FF, LATENT), FF ** -0.5, 0.125, ((0, 1024),))
    cotangent = gaussian(arg_keys[8], (TOKENS, D), 2.0, 12.0, ((0, 16), (1, 64)))
    return dict(tokens=tokens, routes=routes, scores=scores, down_proj=down_proj, up_proj=up_proj, expert_gate=expert_gate, expert_up=expert_up, expert_down=expert_down, cotangent=cotangent)


def slot_table(routes):
    blocks = routes.reshape(N_DP, TOK_ROW * TOP)
    numbers = jnp.arange(EXPERTS, dtype=jnp.int32)
    onehot = (blocks[:, :, None] == numbers[None, None, :]).astype(jnp.int32)
    before = jnp.cumsum(onehot, axis=1, dtype=jnp.int32) - onehot
    position = jnp.sum(before * onehot, axis=2, dtype=jnp.int32)
    block_ids = jnp.arange(N_DP, dtype=jnp.int32)[:, None]
    slot_ids = blocks * (N_DP * CAP) + block_ids * CAP + position
    return slot_ids.reshape(TOKENS * TOP).astype(jnp.int32)


def expert_columns(matrix, number):
    return lax.dynamic_slice_in_dim(matrix, number * FF, FF, 1)


def expert_rows(matrix, number):
    return lax.dynamic_slice_in_dim(matrix, number * FF, FF, 0)


def reference(tokens, routes, scores, down_proj, up_proj, expert_gate, expert_up, expert_down, cotangent):
    latent = jnp.dot(tokens, down_proj, preferred_element_type=jnp.float32).astype(jnp.bfloat16)
    score_vals = scores.astype(jnp.float32)
    share = score_vals / jnp.sum(score_vals, axis=1, keepdims=True)
    slot_ids = slot_table(routes)
    per_expert = N_DP * CAP
    repeated = jnp.repeat(latent, TOP, axis=0)
    slot_rows = jnp.zeros((EXPERTS * per_expert, LATENT), jnp.bfloat16).at[slot_ids].set(repeated)
    slot_rows = slot_rows.reshape(EXPERTS, per_expert, LATENT)
    numbers = jnp.arange(EXPERTS, dtype=jnp.int32)

    def expert_forward(item):
        rows_here, number = item
        gate_val = jnp.dot(rows_here, expert_columns(expert_gate, number), preferred_element_type=jnp.float32)
        lift_val = jnp.dot(rows_here, expert_columns(expert_up, number), preferred_element_type=jnp.float32)
        hidden = (gate_val * jax.nn.sigmoid(gate_val) * lift_val).astype(jnp.bfloat16)
        return jnp.dot(hidden, expert_rows(expert_down, number), preferred_element_type=jnp.float32)

    answers = lax.map(expert_forward, (slot_rows, numbers)).reshape(EXPERTS * per_expert, LATENT)
    per_route = answers[slot_ids].reshape(TOKENS, TOP, LATENT)
    combined = jnp.sum(share[:, :, None] * per_route, axis=1).astype(jnp.bfloat16)
    layer_out = jnp.dot(combined, up_proj, preferred_element_type=jnp.float32).astype(jnp.bfloat16)

    combined_grad = jnp.dot(cotangent, up_proj.T, preferred_element_type=jnp.float32).astype(jnp.bfloat16)
    up_grad = jnp.dot(combined.T, cotangent, preferred_element_type=jnp.float32)
    route_grad = (share[:, :, None] * combined_grad[:, None, :].astype(jnp.float32)).astype(jnp.bfloat16)
    grad_rows = jnp.zeros((EXPERTS * per_expert, LATENT), jnp.bfloat16).at[slot_ids].set(route_grad.reshape(TOKENS * TOP, LATENT))
    grad_rows = grad_rows.reshape(EXPERTS, per_expert, LATENT)

    def expert_backward(item):
        rows_here, grads_here, number = item
        gate_cols = expert_columns(expert_gate, number)
        lift_cols = expert_columns(expert_up, number)
        down_rows = expert_rows(expert_down, number)
        gate_val = jnp.dot(rows_here, gate_cols, preferred_element_type=jnp.float32)
        lift_val = jnp.dot(rows_here, lift_cols, preferred_element_type=jnp.float32)
        sigma_val = jax.nn.sigmoid(gate_val)
        active = gate_val * sigma_val
        hidden = (active * lift_val).astype(jnp.bfloat16)
        hidden_grad = jnp.dot(grads_here, down_rows.T, preferred_element_type=jnp.float32)
        gate_grad = (hidden_grad * lift_val * (sigma_val * (1.0 + gate_val * (1.0 - sigma_val)))).astype(jnp.bfloat16)
        lift_grad = (hidden_grad * active).astype(jnp.bfloat16)
        latent_part = jnp.dot(gate_grad, gate_cols.T, preferred_element_type=jnp.float32) + jnp.dot(lift_grad, lift_cols.T, preferred_element_type=jnp.float32)
        gate_weight = jnp.dot(rows_here.T, gate_grad, preferred_element_type=jnp.float32).astype(jnp.bfloat16)
        lift_weight = jnp.dot(rows_here.T, lift_grad, preferred_element_type=jnp.float32).astype(jnp.bfloat16)
        down_weight = jnp.dot(hidden.T, grads_here, preferred_element_type=jnp.float32).astype(jnp.bfloat16)
        return latent_part, gate_weight, lift_weight, down_weight

    latent_parts, gate_weights, lift_weights, down_weights = lax.map(expert_backward, (slot_rows, grad_rows, numbers))
    latent_parts = latent_parts.reshape(EXPERTS * per_expert, LATENT)[slot_ids].reshape(TOKENS, TOP, LATENT)
    latent_grad = jnp.sum(latent_parts, axis=1).astype(jnp.bfloat16)
    token_grad = jnp.dot(latent_grad, down_proj.T, preferred_element_type=jnp.float32).astype(jnp.bfloat16)
    down_grad = jnp.dot(tokens.T, latent_grad, preferred_element_type=jnp.float32)
    expert_gate_grad = jnp.transpose(gate_weights, (1, 0, 2)).reshape(LATENT, EXPERTS * FF)
    expert_up_grad = jnp.transpose(lift_weights, (1, 0, 2)).reshape(LATENT, EXPERTS * FF)
    expert_down_grad = down_weights.reshape(EXPERTS * FF, LATENT)
    return (layer_out, token_grad, down_grad, up_grad, expert_gate_grad, expert_up_grad, expert_down_grad)
```

```python
import functools

import jax
import jax.numpy as jnp
from jax import lax
from jax.experimental import pallas as pl
from jax.experimental.pallas import tpu as pltpu
from jax.sharding import PartitionSpec as P

MESH = pl.DeviceIdType.MESH
BF = jnp.bfloat16
F32 = jnp.float32
NY = 8
CAP = 12
PAD = 16
LANE = 128


def nn(a, b):
    return jnp.dot(a, b, preferred_element_type=F32)


def nt(a, b):
    return lax.dot_general(a, b, (((1,), (1,)), ((), ())), preferred_element_type=F32)


def tn(a, b):
    return lax.dot_general(a, b, (((0,), (0,)), ((), ())), preferred_element_type=F32)


def kernel(
    ndp, nz, ny,
    tokens, routes, scores, down, up, w_gate, w_up, w_down, cot,
    layer_out, token_grad, down_grad, up_grad, gate_out, lift_out, dexp_out,
    f1, f1r, f2, f2r, b1, b1r, b2, b2r, low,
    pick, wpick, send4, recv4, full, ystage, yrecv, own, back, backr,
    z1, z1r, cf1, cb1, cf, cb, padc, padt, g1, g1r, g2, g2r,
    ssem, rsem, ysend, yrcv, psend, prcv,
):
    dp = lax.axis_index("dp")
    ex = lax.axis_index("expert")
    z, y = ex // ny, ex % ny
    xi, core = dp // 2, dp % 2
    nx = ndp // 2
    tok = tokens.shape[0]
    wide = tokens.shape[1]
    latent = down.shape[1]
    rows = tok // nz
    slots = ndp * PAD
    packed = ndp * CAP
    part = latent // ndp

    def ypeer(d):
        return (dp, z * ny + (y + d + ny) % ny)

    def zpeer(d):
        return (dp, ((z + d + nz) % nz) * ny + y)

    def dpeer(d):
        return ((dp + d + ndp) % ndp, ex)

    def xpeer(d):
        return (((xi + d + nx) % nx) * 2 + core, ex)

    sibling = (xi * 2 + 1 - core, ex)

    pending = []

    def send(src, dst, phase, device):
        pltpu.make_async_remote_copy(
            src_ref=src, dst_ref=dst, send_sem=ssem.at[phase], recv_sem=rsem.at[phase],
            device_id=device, device_id_type=MESH,
        ).start()

    def landed(ref, phase):
        pltpu.make_async_remote_copy(
            src_ref=ref, dst_ref=ref, send_sem=ssem.at[phase], recv_sem=rsem.at[phase],
            device_id=sibling, device_id_type=MESH,
        ).wait_recv()
        pending.append((ref, phase))

    barrier = pltpu.get_barrier_semaphore()
    for d in range(1, ny):
        pl.semaphore_signal(barrier, inc=1, device_id=ypeer(d), device_id_type=MESH)
    for d in range(1, nz):
        pl.semaphore_signal(barrier, inc=1, device_id=zpeer(d), device_id_type=MESH)
    for d in range(1, ndp):
        pl.semaphore_signal(barrier, inc=1, device_id=dpeer(d), device_id_type=MESH)

    part_f = nn(tokens[...], down[...]).astype(BF)
    for q in range(ny):
        f1[q] = part_f[:, q * LANE:(q + 1) * LANE]
    part_b = nt(cot[...], up[...]).astype(BF)
    for q in range(nz):
        b1[q] = part_b[q * rows:(q + 1) * rows]
    pl.semaphore_wait(barrier, ny + nz + ndp - 3)

    for d in range(1, ny):
        send(f1.at[(y + d) % ny], f1r.at[d], 0, ypeer(d))
    for d in range(1, nz):
        send(b1.at[(z + d) % nz], b1r.at[d], 1, zpeer(d))

    r = routes[...]
    s = scores[...].astype(F32)
    share = s / jnp.sum(s, axis=0, keepdims=True)
    target = ((lax.broadcasted_iota(jnp.int32, (ndp, tok), 0) + dp) % ndp) * nz + z
    member = jnp.zeros((ndp, tok), F32)
    weight = jnp.zeros((ndp, tok), F32)
    for k in range(r.shape[0]):
        hit = r[k:k + 1] == target
        member = member + jnp.where(hit, 1.0, 0.0)
        weight = weight + jnp.where(hit, share[k:k + 1], 0.0)
    ahead = lax.broadcasted_iota(jnp.int32, (tok, tok), 0) < lax.broadcasted_iota(jnp.int32, (tok, tok), 1)
    place = nn(member.astype(BF), jnp.where(ahead, 1.0, 0.0).astype(BF))
    place = jnp.where(member > 0.5, place, -1.0).astype(jnp.int32)
    spot = lax.broadcasted_iota(jnp.int32, (PAD, tok), 0)
    for d in range(ndp):
        hit = place[d:d + 1] == spot
        pick[d * PAD:(d + 1) * PAD] = jnp.where(hit, 1.0, 0.0).astype(BF)
        wpick[d * PAD:(d + 1) * PAD] = jnp.where(hit, weight[d:d + 1], 0.0).astype(BF)
    row = lax.broadcasted_iota(jnp.int32, (packed, slots), 0)
    col = lax.broadcasted_iota(jnp.int32, (packed, slots), 1)
    pack = jnp.where((col - row == (PAD - CAP) * (col // PAD)) & (col % PAD < CAP), 1.0, 0.0).astype(BF)
    row = lax.broadcasted_iota(jnp.int32, (slots, packed), 0)
    col = lax.broadcasted_iota(jnp.int32, (slots, packed), 1)
    unpack = jnp.where((row - col == (PAD - CAP) * (row // PAD)) & (row % PAD < CAP), 1.0, 0.0).astype(BF)

    landed(f1r.at[pl.ds(1, ny - 1)], 0)
    total = f1[y].astype(F32)
    for d in range(1, ny):
        total = total + f1r[d].astype(F32)
    total = total.astype(BF)
    for q in range(nz):
        f2[q] = total[q * rows:(q + 1) * rows]
    for d in range(1, nz):
        send(f2.at[(z + d) % nz], f2r.at[d], 2, zpeer(d))
    landed(b1r.at[pl.ds(1, nz - 1)], 1)
    total = b1[z].astype(F32)
    for d in range(1, nz):
        total = total + b1r[d].astype(F32)
    total = total.astype(BF)
    for q in range(ny):
        b2[q] = total[:, q * LANE:(q + 1) * LANE]
    for d in range(1, ny):
        send(b2.at[(y + d) % ny], b2r.at[d], 3, ypeer(d))
    landed(f2r.at[pl.ds(1, nz - 1)], 2)
    total = f2[z].astype(F32)
    for d in range(1, nz):
        total = total + f2r[d].astype(F32)
    low[z, 0] = total.astype(BF)
    landed(b2r.at[pl.ds(1, ny - 1)], 3)
    total = b2[y].astype(F32)
    for d in range(1, ny):
        total = total + b2r[d].astype(F32)
    low[z, 1] = total.astype(BF)
    for d in range(1, nz):
        send(low.at[z], low.at[z], 4, zpeer(d))
    landed(low.at[pl.ds(0, nz - 1)], 4)

    send4[:, 0] = nn(pick[...], low[:, 0].reshape(tok, LANE)).astype(BF).reshape(ndp, PAD, LANE)
    send4[:, 1] = nn(wpick[...], low[:, 1].reshape(tok, LANE)).astype(BF).reshape(ndp, PAD, LANE)
    recv4[0] = send4[0]
    for d in range(1, ndp):
        send(send4.at[d], recv4.at[d], 5, dpeer(d))
    landed(recv4.at[pl.ds(1, ndp - 1)], 5)

    mine = pl.ds(pl.multiple_of(y * LANE, LANE), LANE)
    for p in range(2):
        full[p, :, mine] = nn(pack, recv4[:, p].reshape(slots, LANE)).astype(BF)
    half = ny // 2

    def ring(way, step, p):
        sign = 1 if way == 0 else -1
        at = full.at[p, :, pl.ds(pl.multiple_of(((y - sign * (step - 1) + ny) % ny) * LANE, LANE), LANE)]
        return pltpu.make_async_remote_copy(
            src_ref=at, dst_ref=at,
            send_sem=ysend.at[way, step - 1, p], recv_sem=yrcv.at[way, step - 1, p],
            device_id=ypeer(sign), device_id_type=MESH,
        )

    started = []
    waited = set()

    def ring_wait(way, step, p):
        if (way, step, p) not in waited:
            waited.add((way, step, p))
            ring(way, step, p).wait_recv()

    for step in range(1, half + 1):
        for p in range(2):
            for way in range(2):
                if step == half and way != p:
                    continue
                if step > 1:
                    ring_wait(way, step - 1, p)
                ring(way, step, p).start()
                started.append((way, step, p))
    for p in range(2):
        for way, step, q in started:
            if q == p:
                ring_wait(way, step, q)

    gate = nn(full[0], w_gate[...])
    lift = nn(full[0], w_up[...])
    sigma = jax.nn.sigmoid(gate)
    active = gate * sigma
    hidden = (active * lift).astype(BF)
    own[0] = nn(hidden, w_down[...])

    def lane(q):
        return pl.ds(pl.multiple_of(((q + ny) % ny) * LANE, LANE), LANE)

    def pass_on(way, step, p):
        sign = 1 if way == 0 else -1
        return pltpu.make_async_remote_copy(
            src_ref=ystage.at[way, step - 1, p], dst_ref=yrecv.at[way, step - 1, p],
            send_sem=psend.at[way, step - 1, p], recv_sem=prcv.at[way, step - 1, p],
            device_id=ypeer(sign), device_id_type=MESH,
        )

    def pass_step(step, p):
        for way in range(2):
            sign = 1 if way == 0 else -1
            if step == 1 and way != p:
                continue
            value = own[p, :, lane(y + sign * (half + 1 - step))]
            if step > 2 or (step == 2 and way == p):
                pass_on(way, step - 1, p).wait_recv()
                value = value + yrecv[way, step - 2, p].astype(F32)
            ystage[way, step - 1, p] = value.astype(BF)
            pass_on(way, step, p).start()

    def pass_end(p):
        value = own[p, :, lane(y)]
        for way in range(2):
            if half == 1 and way != p:
                continue
            pass_on(way, half, p).wait_recv()
            value = value + yrecv[way, half - 1, p].astype(F32)
        return value.astype(BF)

    pass_step(1, 0)
    hidden_grad = nt(full[1], w_down[...])
    gate_grad = (hidden_grad * lift * (sigma * (1.0 + gate * (1.0 - sigma)))).astype(BF)
    lift_grad = (hidden_grad * active).astype(BF)
    own[1] = nt(gate_grad, w_gate[...]) + nt(lift_grad, w_up[...])
    pass_step(1, 1)
    work = [
        lambda: gate_out.__setitem__(..., tn(full[0], gate_grad).astype(BF)),
        lambda: lift_out.__setitem__(..., tn(full[0], lift_grad).astype(BF)),
        lambda: dexp_out.__setitem__(..., tn(hidden, full[1]).astype(BF)),
    ]
    for step in range(2, half + 1):
        pass_step(step, 0)
        pass_step(step, 1)
        if work:
            work.pop(0)()
    while work:
        work.pop(0)()

    for p in range(2):
        back[:, p] = nn(unpack, pass_end(p)).astype(BF).reshape(ndp, PAD, LANE)
    backr[0] = back[0]
    for d in range(1, ndp):
        send(back.at[d], backr.at[d], 6, dpeer(-d))
    landed(backr.at[pl.ds(1, ndp - 1)], 6)

    z1[:, 0] = tn(wpick[...], backr[:, 0].reshape(slots, LANE)).astype(BF).reshape(nz, rows, LANE)
    z1[:, 1] = tn(pick[...], backr[:, 1].reshape(slots, LANE)).astype(BF).reshape(nz, rows, LANE)
    for d in range(1, nz):
        send(z1.at[(z + d) % nz], z1r.at[d], 7, zpeer(d))
    padc[...] = jnp.zeros_like(padc)
    padt[...] = jnp.zeros_like(padt)
    padc[:, :wide] = cot[...]
    padt[:, :wide] = tokens[...]
    landed(z1r.at[pl.ds(1, nz - 1)], 7)
    total = z1[z].astype(F32)
    for d in range(1, nz):
        total = total + z1r[d].astype(F32)
    cf1[z] = total[0].astype(BF)
    cb1[:, mine] = total[1].astype(BF)
    for d in range(1, nz):
        send(cf1.at[z], cf1.at[z], 8, zpeer(d))
    for d in range(1, ny):
        send(cb1.at[:, mine], cb1.at[:, mine], 9, ypeer(d))
    landed(cf1.at[pl.ds(0, nz - 1)], 8)
    cf[:, :, mine] = cf1[...]
    for d in range(1, ny):
        send(cf1, cf.at[:, :, mine], 10, ypeer(d))
    landed(cb1.at[:, pl.ds(0, (ny - 1) * LANE)], 9)
    cb[z] = cb1[...]
    for d in range(1, nz):
        send(cb1, cb.at[z], 11, zpeer(d))

    landed(cf.at[:, :, pl.ds(0, (ny - 1) * LANE)], 10)
    whole = cf[...].reshape(tok, latent)
    up_part = tn(whole, padc[...]).astype(BF)
    layer_out[...] = nn(whole, up[...]).astype(BF)
    landed(cb.at[pl.ds(0, nz - 1)], 11)
    whole = cb[...].reshape(tok, latent)
    down_part = tn(whole, padt[...]).astype(BF)
    token_grad[...] = nt(whole, down[...]).astype(BF)
    for q in range(ndp):
        g1[q % 2, q // 2, 0] = up_part[q * part:(q + 1) * part]
        g1[q % 2, q // 2, 1] = down_part[q * part:(q + 1) * part]
    send(g1.at[1 - core], g1r, 12, sibling)
    landed(g1r, 12)
    g2[...] = (g1[core].astype(F32) + g1r[...].astype(F32)).astype(BF)
    for d in range(1, nx):
        send(g2.at[(xi + d) % nx], g2r.at[d], 13, xpeer(d))
    landed(g2r.at[pl.ds(1, nx - 1)], 13)
    total = g2[xi].astype(F32)
    for d in range(1, nx):
        total = total + g2r[d].astype(F32)
    up_grad[...] = total[0, :, :wide]
    down_grad[...] = total[1, :, :wide]

    for ref, phase in pending:
        pltpu.make_async_remote_copy(
            src_ref=ref, dst_ref=ref, send_sem=ssem.at[phase], recv_sem=rsem.at[phase],
            device_id=sibling, device_id_type=MESH,
        ).wait_send()
    for way, step, p in started:
        ring(way, step, p).wait_send()
    for p in range(2):
        for step in range(1, half + 1):
            for way in range(2):
                if not (step == 1 and way != p):
                    pass_on(way, step, p).wait_send()


def make(mesh, ny):
    ndp, nex = mesh.shape["dp"], mesh.shape["expert"]
    nz = nex // ny
    nx = ndp // 2
    half = ny // 2

    def local(tokens, routes, scores, down, up, w_gate, w_up, w_down, cot):
        tok, wide = tokens.shape
        latent, hid = w_gate.shape
        rows, part = tok // nz, latent // ndp
        packed = ndp * CAP
        shape = jax.ShapeDtypeStruct

        def vm(*dims, kind=BF):
            return pltpu.VMEM(dims, kind)

        outs = pl.pallas_call(
            functools.partial(kernel, ndp, nz, ny),
            out_shape=(
                shape((tok, wide), BF),
                shape((tok, wide), BF),
                shape((part, wide), F32),
                shape((part, wide), F32),
                shape((latent, hid), BF),
                shape((latent, hid), BF),
                shape((hid, latent), BF),
            ),
            in_specs=[pl.BlockSpec(memory_space=pltpu.VMEM)] * 9,
            out_specs=[pl.BlockSpec(memory_space=pltpu.VMEM)] * 7,
            scratch_shapes=[
                vm(ny, tok, LANE), vm(ny, tok, LANE), vm(nz, rows, LANE), vm(nz, rows, LANE),
                vm(nz, rows, latent), vm(nz, rows, latent), vm(ny, rows, LANE), vm(ny, rows, LANE),
                vm(nz, 2, rows, LANE),
                vm(ndp * PAD, tok), vm(ndp * PAD, tok),
                vm(ndp, 2, PAD, LANE), vm(ndp, 2, PAD, LANE),
                vm(2, packed, latent),
                vm(2, half, 2, packed, LANE), vm(2, half, 2, packed, LANE),
                vm(2, packed, latent, kind=F32),
                vm(ndp, 2, PAD, LANE), vm(ndp, 2, PAD, LANE),
                vm(nz, 2, rows, LANE), vm(nz, 2, rows, LANE),
                vm(nz, rows, LANE), vm(rows, latent), vm(nz, rows, latent), vm(nz, rows, latent),
                vm(tok, LANE), vm(tok, LANE),
                vm(2, nx, 2, part, LANE), vm(nx, 2, part, LANE), vm(nx, 2, part, LANE), vm(nx, 2, part, LANE),
                pltpu.SemaphoreType.DMA((14,)), pltpu.SemaphoreType.DMA((14,)),
                pltpu.SemaphoreType.DMA((2, half, 2)), pltpu.SemaphoreType.DMA((2, half, 2)),
                pltpu.SemaphoreType.DMA((2, half, 2)), pltpu.SemaphoreType.DMA((2, half, 2)),
            ],
            compiler_params=pltpu.CompilerParams(
                collective_id=0, has_side_effects=True, vmem_limit_bytes=56 * 1024 * 1024,
            ),
        )(tokens, routes.T, scores.T, down, up, w_gate, w_up, w_down, cot)
        layer_out, token_grad, down_grad, up_grad, gate_out, lift_out, dexp_out = outs
        return layer_out, token_grad, down_grad.T, up_grad, gate_out, lift_out, dexp_out

    return jax.shard_map(
        local, mesh=mesh,
        in_specs=(
            P("dp", "expert"), P("dp", None), P("dp", None), P("expert", None), P(None, "expert"),
            P(None, ("dp", "expert")), P(None, ("dp", "expert")), P(("dp", "expert"), None), P("dp", "expert"),
        ),
        out_specs=(
            P("dp", "expert"), P("dp", "expert"), P("expert", "dp"), P("dp", "expert"),
            P(None, ("dp", "expert")), P(None, ("dp", "expert")), P(("dp", "expert"), None),
        ),
        check_vma=False,
    )


def solution(mesh):
    return make(mesh, NY)
```

```python
import functools

import jax
import jax.numpy as jnp
from jax import lax
from jax.experimental import pallas as pl
from jax.experimental.pallas import tpu as pltpu
from jax.sharding import PartitionSpec as P

MESH = pl.DeviceIdType.MESH
BF = jnp.bfloat16
F32 = jnp.float32
NY = 8
CAP = 12
PAD = 16
LANE = 128
CUT = 2


def nn(a, b):
    return jnp.dot(a, b, preferred_element_type=F32)


def nt(a, b):
    return lax.dot_general(a, b, (((1,), (1,)), ((), ())), preferred_element_type=F32)


def tn(a, b):
    return lax.dot_general(a, b, (((0,), (0,)), ((), ())), preferred_element_type=F32)


def kernel(
    ndp, nz, ny,
    hbm_tokens, routes, scores, hbm_proj, hbm_back, hbm_gate, hbm_up, hbm_down, hbm_cot,
    layer_out, token_grad, down_grad, up_grad, hbm_gate_out, hbm_lift_out, hbm_dexp_out,
    tokens, down, up, cot, w_gate, w_up, w_down, gate_out, lift_out, dexp_out, isem, osem,
    f1, f1r, f2, f2r, b1, b1r, b2, b2r, low,
    pick, send4, recv4, full, ystage, yrecv, own, back, backr,
    z1, z1r, cf1, cb1, cf, cb, padded, g1, g1r, g2, g2r,
    ssem, rsem, ysend, yrcv, psend, prcv,
):
    dp = lax.axis_index("dp")
    ex = lax.axis_index("expert")
    z, y = ex // ny, ex % ny
    xi, core = dp // 2, dp % 2
    nx = ndp // 2
    wide, tok = tokens.shape
    latent = down.shape[1]
    rows = tok // nz
    slots = ndp * PAD
    packed = ndp * CAP

    def ypeer(d):
        return (dp, z * ny + (y + d + ny) % ny)

    def zpeer(d):
        return (dp, ((z + d + nz) % nz) * ny + y)

    def dpeer(d):
        return ((dp + d + ndp) % ndp, ex)

    def xpeer(d):
        return (((xi + d + nx) % nx) * 2 + core, ex)

    def far(count):
        return sorted(range(1, count), key=lambda d: -min(d, count - d))

    sibling = (xi * 2 + 1 - core, ex)

    pending = []

    def finish():
        for wait in pending:
            wait()

    fetch = [
        pltpu.make_async_copy(src, dst, isem.at[n])
        for n, (src, dst) in enumerate((
            (hbm_tokens, tokens), (hbm_proj, down), (hbm_cot, cot), (hbm_back, up),
            (hbm_gate, w_gate), (hbm_up, w_up), (hbm_down, w_down),
        ))
    ]
    for copy in fetch:
        copy.start()

    def send(src, dst, phase, device):
        pltpu.make_async_remote_copy(
            src_ref=src, dst_ref=dst, send_sem=ssem.at[phase], recv_sem=rsem.at[phase],
            device_id=device, device_id_type=MESH,
        ).start()

    def landed(ref, phase):
        whole = pltpu.make_async_remote_copy(
            src_ref=ref, dst_ref=ref, send_sem=ssem.at[phase], recv_sem=rsem.at[phase],
            device_id=sibling, device_id_type=MESH,
        )
        whole.wait_recv()
        pending.append(whole.wait_send)

    barrier = pltpu.get_barrier_semaphore()
    for d in range(1, ny):
        pl.semaphore_signal(barrier, inc=1, device_id=ypeer(d), device_id_type=MESH)
    for d in range(1, nz):
        pl.semaphore_signal(barrier, inc=1, device_id=zpeer(d), device_id_type=MESH)
    for d in range(1, ndp):
        pl.semaphore_signal(barrier, inc=1, device_id=dpeer(d), device_id_type=MESH)

    fetch[0].wait()
    fetch[1].wait()
    part = tn(tokens[...], down[...]).astype(BF)
    for q in range(ny):
        f1[q] = part[:, q * LANE:(q + 1) * LANE]
    pl.semaphore_wait(barrier, ny + nz + ndp - 3)
    for d in far(ny):
        send(f1.at[(y + d) % ny], f1r.at[d], 0, ypeer(d))
    fetch[2].wait()
    fetch[3].wait()
    part = tn(cot[...], up[...]).astype(BF)
    for q in range(nz):
        b1[q] = part[q * rows:(q + 1) * rows]
    for d in far(nz):
        send(b1.at[(z + d) % nz], b1r.at[d], 1, zpeer(d))

    r = routes[...]
    s = scores[...].astype(F32)
    share = s / jnp.sum(s, axis=0, keepdims=True)
    target = lax.broadcasted_iota(jnp.int32, (ndp, tok), 0) + dp
    target = jnp.where(target >= ndp, target - ndp, target) * nz + z
    member = jnp.zeros((ndp, tok), F32)
    weight = jnp.zeros((ndp, tok), F32)
    for k in range(r.shape[0]):
        hit = r[k:k + 1] == target
        member = member + jnp.where(hit, 1.0, 0.0)
        weight = weight + jnp.where(hit, share[k:k + 1], 0.0)
    ahead = lax.broadcasted_iota(jnp.int32, (tok, tok), 0) < lax.broadcasted_iota(jnp.int32, (tok, tok), 1)
    place = nn(member.astype(BF), jnp.where(ahead, 1.0, 0.0).astype(BF))
    place = jnp.where(member > 0.5, place, -1.0).astype(jnp.int32)
    spot = lax.broadcasted_iota(jnp.int32, (PAD, tok), 0)
    for d in range(ndp):
        hit = place[d:d + 1] == spot
        pick[0, d * PAD:(d + 1) * PAD] = jnp.where(hit, 1.0, 0.0).astype(BF)
        pick[1, d * PAD:(d + 1) * PAD] = jnp.where(hit, weight[d:d + 1], 0.0).astype(BF)
    row = lax.broadcasted_iota(jnp.int32, (packed, slots), 0)
    col = lax.broadcasted_iota(jnp.int32, (packed, slots), 1)
    pack = jnp.where((col - row == (col >> 4) * (PAD - CAP)) & ((col & (PAD - 1)) < CAP), 1.0, 0.0).astype(BF)
    row = lax.broadcasted_iota(jnp.int32, (slots, packed), 0)
    col = lax.broadcasted_iota(jnp.int32, (slots, packed), 1)
    unpack = jnp.where((row - col == (row >> 4) * (PAD - CAP)) & ((row & (PAD - 1)) < CAP), 1.0, 0.0).astype(BF)
    padded[...] = jnp.zeros_like(padded)
    padded[0, :, :wide] = cot[...].T
    padded[1, :, :wide] = tokens[...].T

    def gathered(first, others, count):
        total = first.astype(F32)
        for d in range(1, count):
            total = total + others[d].astype(F32)
        return total

    landed(f1r.at[pl.ds(1, ny - 1)], 0)
    total = gathered(f1[y], f1r, ny).astype(BF)
    for q in range(nz):
        f2[q] = total[q * rows:(q + 1) * rows]
    for d in far(nz):
        send(f2.at[(z + d) % nz], f2r.at[d], 2, zpeer(d))
    landed(b1r.at[pl.ds(1, nz - 1)], 1)
    total = gathered(b1[z], b1r, nz).astype(BF)
    for q in range(ny):
        b2[q] = total[:, q * LANE:(q + 1) * LANE]
    for d in far(ny):
        send(b2.at[(y + d) % ny], b2r.at[d], 3, ypeer(d))
    landed(f2r.at[pl.ds(1, nz - 1)], 2)
    low[0, z] = gathered(f2[z], f2r, nz).astype(BF)
    for d in far(nz):
        send(low.at[0, z], low.at[0, z], 4, zpeer(d))
    landed(b2r.at[pl.ds(1, ny - 1)], 3)
    low[1, z] = gathered(b2[y], b2r, ny).astype(BF)
    for d in far(nz):
        send(low.at[1, z], low.at[1, z], 5, zpeer(d))

    for p in range(2):
        landed(low.at[p, pl.ds(0, nz - 1)], 4 + p)
        value = nn(pick[p], low[p].reshape(tok, LANE))
        send4[p] = value.astype(BF).reshape(ndp, PAD, LANE)
        for d in far(ndp):
            send(send4.at[p, d], recv4.at[p, d], 6 + p, dpeer(d))
        recv4[p, 0] = send4[p, 0]

    mine = pl.ds(pl.multiple_of(y * LANE, LANE), LANE)
    half = ny // 2
    piece = packed // CUT

    def lane(q):
        return pl.ds(pl.multiple_of(((q + ny) % ny) * LANE, LANE), LANE)

    def skips(way, k):
        return way != k % 2

    def ring(way, step, k):
        sign = 1 if way == 0 else -1
        at = full.at[k // CUT, pl.ds(k % CUT * piece, piece), lane(y - sign * (step - 1))]
        return pltpu.make_async_remote_copy(
            src_ref=at, dst_ref=at,
            send_sem=ysend.at[way, step - 1, k], recv_sem=yrcv.at[way, step - 1, k],
            device_id=ypeer(sign), device_id_type=MESH,
        )

    waited = set()

    def ring_wait(way, step, k):
        if (way, step, k) not in waited:
            waited.add((way, step, k))
            ring(way, step, k).wait_recv()

    def ring_step(step, p):
        for k in range(p * CUT, (p + 1) * CUT):
            for way in range(2):
                if step == half and skips(way, k):
                    continue
                if step > 1:
                    ring_wait(way, step - 1, k)
                ring(way, step, k).start()
                pending.append(ring(way, step, k).wait_send)

    def ring_end(p):
        for step in range(1, half + 1):
            for k in range(p * CUT, (p + 1) * CUT):
                for way in range(2):
                    if not (step == half and skips(way, k)):
                        ring_wait(way, step, k)

    for p in range(2):
        landed(recv4.at[p, pl.ds(1, ndp - 1)], 6 + p)
        full[p, :, mine] = nn(pack, recv4[p].reshape(slots, LANE)).astype(BF)
        ring_step(1, p)
    for step in range(2, half + 1):
        for p in range(2):
            ring_step(step, p)
    ring_end(0)

    for copy in fetch[4:]:
        copy.wait()
    gate = nn(full[0], w_gate[...])
    lift = nn(full[0], w_up[...])
    sigma = jax.nn.sigmoid(gate)
    active = gate * sigma
    hidden = (active * lift).astype(BF)
    own[0] = nn(hidden, w_down[...])

    def pass_on(way, step, k):
        sign = 1 if way == 0 else -1
        return pltpu.make_async_remote_copy(
            src_ref=ystage.at[way, step - 1, k], dst_ref=yrecv.at[way, step - 1, k],
            send_sem=psend.at[way, step - 1, k], recv_sem=prcv.at[way, step - 1, k],
            device_id=ypeer(sign), device_id_type=MESH,
        )

    def pass_step(step, p):
        for k in range(p * CUT, (p + 1) * CUT):
            for way in range(2):
                sign = 1 if way == 0 else -1
                if step == 1 and skips(way, k):
                    continue
                value = own[p, pl.ds(k % CUT * piece, piece), lane(y + sign * (half + 1 - step))]
                if step > 2 or (step == 2 and not skips(way, k)):
                    pass_on(way, step - 1, k).wait_recv()
                    value = value + yrecv[way, step - 2, k].astype(F32)
                ystage[way, step - 1, k] = value.astype(BF)
                pass_on(way, step, k).start()
                pending.append(pass_on(way, step, k).wait_send)

    def pass_end(p):
        parts = []
        for k in range(p * CUT, (p + 1) * CUT):
            value = own[p, pl.ds(k % CUT * piece, piece), lane(y)]
            for way in range(2):
                if half == 1 and skips(way, k):
                    continue
                pass_on(way, half, k).wait_recv()
                value = value + yrecv[way, half - 1, k].astype(F32)
            parts.append(value.astype(BF))
        return jnp.concatenate(parts, axis=0)

    pass_step(1, 0)
    ring_end(1)
    hidden_grad = nt(full[1], w_down[...])
    gate_grad = (hidden_grad * lift * (sigma * (1.0 + gate * (1.0 - sigma)))).astype(BF)
    lift_grad = (hidden_grad * active).astype(BF)
    own[1] = nt(gate_grad, w_gate[...]) + nt(lift_grad, w_up[...])
    pass_step(1, 1)
    work = [
        (gate_out, hbm_gate_out, lambda: tn(full[0], gate_grad)),
        (lift_out, hbm_lift_out, lambda: tn(full[0], lift_grad)),
        (dexp_out, hbm_dexp_out, lambda: tn(hidden, full[1])),
    ]

    def do_work():
        held, out, product = work.pop(0)
        held[...] = product().astype(BF)
        copy = pltpu.make_async_copy(held, out, osem.at[len(work)])
        copy.start()
        pending.append(copy.wait)

    for step in range(2, half + 1):
        pass_step(step, 0)
        pass_step(step, 1)
        if work:
            do_work()
    while work:
        do_work()

    for p in range(2):
        back[p] = nn(unpack, pass_end(p)).astype(BF).reshape(ndp, PAD, LANE)
        for d in far(ndp):
            send(back.at[p, d], backr.at[p, d], 8 + p, dpeer(-d))
        backr[p, 0] = back[p, 0]

    for p in range(2):
        landed(backr.at[p, pl.ds(1, ndp - 1)], 8 + p)
        value = tn(pick[1 - p], backr[p].reshape(slots, LANE))
        z1[p] = value.astype(BF).reshape(nz, rows, LANE)
        for d in far(nz):
            send(z1.at[p, (z + d) % nz], z1r.at[p, d], 10 + p, zpeer(d))
    landed(z1r.at[0, pl.ds(1, nz - 1)], 10)
    cf1[z] = gathered(z1[0, z], z1r.at[0], nz).astype(BF)
    for d in far(nz):
        send(cf1.at[z], cf1.at[z], 12, zpeer(d))
    landed(z1r.at[1, pl.ds(1, nz - 1)], 11)
    cb1[:, mine] = gathered(z1[1, z], z1r.at[1], nz).astype(BF)
    for d in far(ny):
        send(cb1.at[:, mine], cb1.at[:, mine], 13, ypeer(d))
    landed(cf1.at[pl.ds(0, nz - 1)], 12)
    for d in far(ny):
        send(cf1, cf.at[:, :, mine], 14, ypeer(d))
    cf[:, :, mine] = cf1[...]
    landed(cb1.at[:, pl.ds(0, (ny - 1) * LANE)], 13)
    for d in far(nz):
        send(cb1, cb.at[z], 15, zpeer(d))
    cb[z] = cb1[...]

    share_rows = latent // ndp
    for p, (ref, wait) in enumerate((
        (cf, cf.at[:, :, pl.ds(0, (ny - 1) * LANE)]), (cb, cb.at[pl.ds(0, nz - 1)]),
    )):
        landed(wait, 14 + p)
        value = tn(ref[...].reshape(tok, latent), padded[p]).astype(BF)
        for q in range(ndp):
            g1[p, q % 2, q // 2] = value[q * share_rows:(q + 1) * share_rows]
        send(g1.at[p, 1 - core], g1r.at[p], 16 + p, sibling)
    for p in range(2):
        landed(g1r.at[p], 16 + p)
        g2[p] = (g1[p, core].astype(F32) + g1r[p].astype(F32)).astype(BF)
        for d in far(nx):
            send(g2.at[p, (xi + d) % nx], g2r.at[p, d], 18 + p, xpeer(d))
    layer_out[...] = nt(up[...], cf[...].reshape(tok, latent)).astype(BF)
    token_grad[...] = nt(down[...], cb[...].reshape(tok, latent)).astype(BF)
    for p, out in enumerate((up_grad, down_grad)):
        landed(g2r.at[p, pl.ds(1, nx - 1)], 18 + p)
        out[...] = gathered(g2[p, xi], g2r.at[p], nx)[:, :wide]
    finish()


def hand_over(*refs):
    count = (len(refs) - 2) // 3
    given, outs, held = refs[:count], refs[count:2 * count], refs[2 * count:3 * count]
    arrived, left = refs[3 * count:]
    ins = [pltpu.make_async_copy(given[n], held[n], arrived.at[n]) for n in range(count)]
    out = [pltpu.make_async_copy(held[n], outs[n], left.at[n]) for n in range(count)]
    for copy in ins:
        copy.start()
    for n in range(count):
        ins[n].wait()
        out[n].start()
    for copy in out:
        copy.wait()


def make(mesh, ny):
    ndp, nex = mesh.shape["dp"], mesh.shape["expert"]
    nz = nex // ny
    nx = ndp // 2
    half = ny // 2

    def local(tokens, routes, scores, down, up, w_gate, w_up, w_down, cot):
        tokens, cot, up = tokens.T, cot.T, up.T
        wide, tok = tokens.shape
        latent, hid = w_gate.shape
        rows, part = tok // nz, latent // ndp
        packed = ndp * CAP
        shape = jax.ShapeDtypeStruct
        inside = pl.BlockSpec(memory_space=pltpu.VMEM)
        outside = pl.BlockSpec(memory_space=pl.ANY)

        def vm(*dims, kind=BF):
            return pltpu.VMEM(dims, kind)

        outs = pl.pallas_call(
            functools.partial(kernel, ndp, nz, ny),
            out_shape=(
                shape((wide, tok), BF),
                shape((wide, tok), BF),
                shape((part, wide), F32),
                shape((part, wide), F32),
                shape((latent, hid), BF),
                shape((latent, hid), BF),
                shape((hid, latent), BF),
            ),
            in_specs=[outside] + [inside] * 2 + [outside] * 6,
            out_specs=[inside] * 4 + [outside] * 3,
            scratch_shapes=[
                vm(wide, tok), vm(wide, latent), vm(wide, latent), vm(wide, tok),
                vm(latent, hid), vm(latent, hid), vm(hid, latent),
                vm(latent, hid), vm(latent, hid), vm(hid, latent),
                pltpu.SemaphoreType.DMA((7,)), pltpu.SemaphoreType.DMA((3,)),
                vm(ny, tok, LANE), vm(ny, tok, LANE), vm(nz, rows, LANE), vm(nz, rows, LANE),
                vm(nz, rows, latent), vm(nz, rows, latent), vm(ny, rows, LANE), vm(ny, rows, LANE),
                vm(2, nz, rows, LANE),
                vm(2, ndp * PAD, tok),
                vm(2, ndp, PAD, LANE), vm(2, ndp, PAD, LANE),
                vm(2, packed, latent),
                vm(2, half, 2 * CUT, packed // CUT, LANE), vm(2, half, 2 * CUT, packed // CUT, LANE),
                vm(2, packed, latent, kind=F32),
                vm(2, ndp, PAD, LANE), vm(2, ndp, PAD, LANE),
                vm(2, nz, rows, LANE), vm(2, nz, rows, LANE),
                vm(nz, rows, LANE), vm(rows, latent), vm(nz, rows, latent), vm(nz, rows, latent),
                vm(2, tok, LANE),
                vm(2, 2, nx, part, LANE), vm(2, nx, part, LANE), vm(2, nx, part, LANE), vm(2, nx, part, LANE),
                pltpu.SemaphoreType.DMA((20,)), pltpu.SemaphoreType.DMA((20,)),
                pltpu.SemaphoreType.DMA((2, half, 2 * CUT)), pltpu.SemaphoreType.DMA((2, half, 2 * CUT)),
                pltpu.SemaphoreType.DMA((2, half, 2 * CUT)), pltpu.SemaphoreType.DMA((2, half, 2 * CUT)),
            ],
            compiler_params=pltpu.CompilerParams(
                collective_id=0, has_side_effects=True, vmem_limit_bytes=56 * 1024 * 1024,
            ),
        )(tokens, routes.T, scores.T, down, up, w_gate, w_up, w_down, cot)
        layer_out, token_grad, down_grad, up_grad, gate_out, lift_out, dexp_out = pl.pallas_call(
            hand_over,
            out_shape=[shape(out.shape, out.dtype) for out in outs],
            in_specs=[outside] * len(outs),
            out_specs=[outside] * len(outs),
            scratch_shapes=[vm(*out.shape, kind=out.dtype) for out in outs] + [
                pltpu.SemaphoreType.DMA((len(outs),)), pltpu.SemaphoreType.DMA((len(outs),)),
            ],
            compiler_params=pltpu.CompilerParams(vmem_limit_bytes=58 * 1024 * 1024),
        )(*outs)
        return layer_out.T, token_grad.T, down_grad.T, up_grad, gate_out, lift_out, dexp_out

    return jax.shard_map(
        local, mesh=mesh,
        in_specs=(
            P("dp", "expert"), P("dp", None), P("dp", None), P("expert", None), P(None, "expert"),
            P(None, ("dp", "expert")), P(None, ("dp", "expert")), P(("dp", "expert"), None), P("dp", "expert"),
        ),
        out_specs=(
            P("dp", "expert"), P("dp", "expert"), P("expert", "dp"), P("dp", "expert"),
            P(None, ("dp", "expert")), P(None, ("dp", "expert")), P(("dp", "expert"), None),
        ),
        check_vma=False,
    )


def solution(mesh):
    return make(mesh, NY)
```

```python
import functools

import jax
import jax.numpy as jnp
from jax import lax
from jax.experimental import pallas as pl
from jax.experimental.pallas import tpu as pltpu
from jax.sharding import PartitionSpec as P

MESH = pl.DeviceIdType.MESH
BF = jnp.bfloat16
F32 = jnp.float32
NY = 8
CAP = 12
PAD = 16
LANE = 128
CUT = 1


def nn(a, b):
    return jnp.dot(a, b, preferred_element_type=F32)


def nt(a, b):
    return lax.dot_general(a, b, (((1,), (1,)), ((), ())), preferred_element_type=F32)


def tn(a, b):
    return lax.dot_general(a, b, (((0,), (0,)), ((), ())), preferred_element_type=F32)


def kernel(
    ndp, nz, ny,
    hbm_tokens, routes, scores, hbm_proj, hbm_back, hbm_gate, hbm_up, hbm_down, hbm_cot,
    layer_out, token_grad, down_grad, up_grad, hbm_gate_out, hbm_lift_out, hbm_dexp_out,
    tokens, down, up, cot, w_gate, w_up, w_down, gate_out, lift_out, dexp_out, isem, osem,
    f1, f1r, f2, f2r, b1, b1r, b2, b2r, low,
    pick, send4, recv4, full, ystage, yrecv, own, back, backr,
    z1, z1r, cf1, cb1, cf, cb, padded, g1, g1r, g2, g2r,
    ssem, rsem, ysend, yrcv, psend, prcv,
):
    dp = lax.axis_index("dp")
    ex = lax.axis_index("expert")
    z, y = ex // ny, ex % ny
    xi, core = dp // 2, dp % 2
    nx = ndp // 2
    wide, tok = tokens.shape
    latent = down.shape[1]
    rows = tok // nz
    slots = ndp * PAD
    packed = ndp * CAP

    def ypeer(d):
        return (dp, z * ny + (y + d + ny) % ny)

    def zpeer(d):
        return (dp, ((z + d + nz) % nz) * ny + y)

    def dpeer(d):
        return ((dp + d + ndp) % ndp, ex)

    def xpeer(d):
        return (((xi + d + nx) % nx) * 2 + core, ex)

    def far(count):
        return sorted(range(1, count), key=lambda d: -min(d, count - d))

    sibling = (xi * 2 + 1 - core, ex)

    pending = []

    def finish():
        for wait in pending:
            wait()

    fetch = [
        pltpu.make_async_copy(src, dst, isem.at[n])
        for n, (src, dst) in enumerate((
            (hbm_tokens, tokens), (hbm_proj, down), (hbm_cot, cot), (hbm_back, up),
            (hbm_gate, w_gate), (hbm_up, w_up), (hbm_down, w_down),
        ))
    ]
    for copy in fetch:
        copy.start()

    def send(src, dst, phase, device):
        pltpu.make_async_remote_copy(
            src_ref=src, dst_ref=dst, send_sem=ssem.at[phase], recv_sem=rsem.at[phase],
            device_id=device, device_id_type=MESH,
        ).start()

    def landed(ref, phase):
        whole = pltpu.make_async_remote_copy(
            src_ref=ref, dst_ref=ref, send_sem=ssem.at[phase], recv_sem=rsem.at[phase],
            device_id=sibling, device_id_type=MESH,
        )
        whole.wait_recv()
        pending.append(whole.wait_send)

    barrier = pltpu.get_barrier_semaphore()
    for d in range(1, ny):
        pl.semaphore_signal(barrier, inc=1, device_id=ypeer(d), device_id_type=MESH)
    for d in range(1, nz):
        pl.semaphore_signal(barrier, inc=1, device_id=zpeer(d), device_id_type=MESH)
    for d in range(1, ndp):
        pl.semaphore_signal(barrier, inc=1, device_id=dpeer(d), device_id_type=MESH)

    fetch[0].wait()
    fetch[1].wait()
    part = tn(tokens[...], down[...]).astype(BF)
    for q in range(ny):
        f1[q] = part[:, q * LANE:(q + 1) * LANE]
    pl.semaphore_wait(barrier, ny + nz + ndp - 3)
    for d in far(ny):
        send(f1.at[(y + d) % ny], f1r.at[d], 0, ypeer(d))
    fetch[2].wait()
    fetch[3].wait()
    part = tn(cot[...], up[...]).astype(BF)
    for q in range(nz):
        b1[q] = part[q * rows:(q + 1) * rows]
    for d in far(nz):
        send(b1.at[(z + d) % nz], b1r.at[d], 1, zpeer(d))

    r = routes[...]
    s = scores[...].astype(F32)
    share = s / jnp.sum(s, axis=0, keepdims=True)
    target = lax.broadcasted_iota(jnp.int32, (ndp, tok), 0) + dp
    target = jnp.where(target >= ndp, target - ndp, target) * nz + z
    member = jnp.zeros((ndp, tok), F32)
    weight = jnp.zeros((ndp, tok), F32)
    for k in range(r.shape[0]):
        hit = r[k:k + 1] == target
        member = member + jnp.where(hit, 1.0, 0.0)
        weight = weight + jnp.where(hit, share[k:k + 1], 0.0)
    ahead = lax.broadcasted_iota(jnp.int32, (tok, tok), 0) < lax.broadcasted_iota(jnp.int32, (tok, tok), 1)
    place = nn(member.astype(BF), jnp.where(ahead, 1.0, 0.0).astype(BF))
    place = jnp.where(member > 0.5, place, -1.0).astype(jnp.int32)
    spot = lax.broadcasted_iota(jnp.int32, (PAD, tok), 0)
    for d in range(ndp):
        hit = place[d:d + 1] == spot
        pick[0, d * PAD:(d + 1) * PAD] = jnp.where(hit, 1.0, 0.0).astype(BF)
        pick[1, d * PAD:(d + 1) * PAD] = jnp.where(hit, weight[d:d + 1], 0.0).astype(BF)
    row = lax.broadcasted_iota(jnp.int32, (packed, slots), 0)
    col = lax.broadcasted_iota(jnp.int32, (packed, slots), 1)
    pack = jnp.where((col - row == (col >> 4) * (PAD - CAP)) & ((col & (PAD - 1)) < CAP), 1.0, 0.0).astype(BF)
    row = lax.broadcasted_iota(jnp.int32, (slots, packed), 0)
    col = lax.broadcasted_iota(jnp.int32, (slots, packed), 1)
    unpack = jnp.where((row - col == (row >> 4) * (PAD - CAP)) & ((row & (PAD - 1)) < CAP), 1.0, 0.0).astype(BF)
    padded[...] = jnp.zeros_like(padded)
    padded[0, :, :wide] = cot[...].T
    padded[1, :, :wide] = tokens[...].T

    def gathered(first, others, count):
        total = first.astype(F32)
        for d in range(1, count):
            total = total + others[d].astype(F32)
        return total

    landed(f1r.at[pl.ds(1, ny - 1)], 0)
    total = gathered(f1[y], f1r, ny).astype(BF)
    for q in range(nz):
        f2[q] = total[q * rows:(q + 1) * rows]
    for d in far(nz):
        send(f2.at[(z + d) % nz], f2r.at[d], 2, zpeer(d))
    landed(b1r.at[pl.ds(1, nz - 1)], 1)
    total = gathered(b1[z], b1r, nz).astype(BF)
    for q in range(ny):
        b2[q] = total[:, q * LANE:(q + 1) * LANE]
    for d in far(ny):
        send(b2.at[(y + d) % ny], b2r.at[d], 3, ypeer(d))
    landed(f2r.at[pl.ds(1, nz - 1)], 2)
    low[0, z] = gathered(f2[z], f2r, nz).astype(BF)
    for d in far(nz):
        send(low.at[0, z], low.at[0, z], 4, zpeer(d))
    landed(b2r.at[pl.ds(1, ny - 1)], 3)
    low[1, z] = gathered(b2[y], b2r, ny).astype(BF)
    for d in far(nz):
        send(low.at[1, z], low.at[1, z], 5, zpeer(d))

    for p in range(2):
        landed(low.at[p, pl.ds(0, nz - 1)], 4 + p)
        value = nn(pick[p], low[p].reshape(tok, LANE))
        send4[p] = value.astype(BF).reshape(ndp, PAD, LANE)
        for d in far(ndp):
            send(send4.at[p, d], recv4.at[p, d], 6 + p, dpeer(d))
        recv4[p, 0] = send4[p, 0]

    mine = pl.ds(pl.multiple_of(y * LANE, LANE), LANE)
    piece = packed // CUT

    def lane(q):
        return pl.ds(pl.multiple_of(((q + ny) % ny) * LANE, LANE), LANE)

    def pieces(p):
        return [(k, way) for k in range(p * CUT, (p + 1) * CUT) for way in range(2)]

    def hop(way, leg, k):
        sign = 1 if way == 0 else -1
        source = y if leg < 2 else y - 2 * sign
        at = full.at[k // CUT, pl.ds(k % CUT * piece, piece), lane(source)]
        return pltpu.make_async_remote_copy(
            src_ref=at, dst_ref=at,
            send_sem=ysend.at[way, leg, k], recv_sem=yrcv.at[way, leg, k],
            device_id=ypeer(sign * (1 + leg % 2)), device_id_type=MESH,
        )

    def start(copy):
        copy.start()
        pending.append(copy.wait_send)

    for p in range(2):
        landed(recv4.at[p, pl.ds(1, ndp - 1)], 6 + p)
        full[p, :, mine] = nn(pack, recv4[p].reshape(slots, LANE)).astype(BF)
        for leg in (1, 0):
            for k, way in pieces(p):
                start(hop(way, leg, k))
    for p in range(2):
        for k, way in pieces(p):
            hop(way, 1, k).wait_recv()
            if way == k % 2:
                start(hop(way, 3, k))
            start(hop(way, 2, k))

    def gather_end(p):
        for k, way in pieces(p):
            hop(way, 0, k).wait_recv()
            hop(way, 2, k).wait_recv()
            if way == k % 2:
                hop(way, 3, k).wait_recv()

    gather_end(0)

    for copy in fetch[4:]:
        copy.wait()
    gate = nn(full[0], w_gate[...])
    lift = nn(full[0], w_up[...])
    sigma = jax.nn.sigmoid(gate)
    active = gate * sigma
    hidden = (active * lift).astype(BF)
    own[0] = nn(hidden, w_down[...])

    def block(p, k, to):
        return own[p, pl.ds(k % CUT * piece, piece), lane(to)]

    def pass_on(way, leg, k):
        sign = 1 if way == 0 else -1
        return pltpu.make_async_remote_copy(
            src_ref=ystage.at[way, leg, k], dst_ref=yrecv.at[way, leg, k],
            send_sem=psend.at[way, leg, k], recv_sem=prcv.at[way, leg, k],
            device_id=ypeer(sign * (1 + leg % 2)), device_id_type=MESH,
        )

    def pass_first(p):
        for k, way in pieces(p):
            sign = 1 if way == 0 else -1
            if way == k % 2:
                ystage[way, 3, k] = block(p, k, y + 4 * sign).astype(BF)
                start(pass_on(way, 3, k))
            ystage[way, 2, k] = block(p, k, y + 3 * sign).astype(BF)
            start(pass_on(way, 2, k))
        for k, way in pieces(p):
            sign = 1 if way == 0 else -1
            ystage[way, 0, k] = block(p, k, y + sign).astype(BF)
            start(pass_on(way, 0, k))

    def pass_second(p):
        for k, way in pieces(p):
            sign = 1 if way == 0 else -1
            value = block(p, k, y + 2 * sign)
            pass_on(way, 2, k).wait_recv()
            value = value + yrecv[way, 2, k].astype(F32)
            if way == k % 2:
                pass_on(way, 3, k).wait_recv()
                value = value + yrecv[way, 3, k].astype(F32)
            ystage[way, 1, k] = value.astype(BF)
            start(pass_on(way, 1, k))

    def pass_end(p):
        parts = []
        for k in range(p * CUT, (p + 1) * CUT):
            value = block(p, k, y)
            for way in range(2):
                for leg in (0, 1):
                    pass_on(way, leg, k).wait_recv()
                    value = value + yrecv[way, leg, k].astype(F32)
            parts.append(value.astype(BF))
        return jnp.concatenate(parts, axis=0)

    pass_first(0)
    gather_end(1)
    hidden_grad = nt(full[1], w_down[...])
    gate_grad = (hidden_grad * lift * (sigma * (1.0 + gate * (1.0 - sigma)))).astype(BF)
    lift_grad = (hidden_grad * active).astype(BF)
    own[1] = nt(gate_grad, w_gate[...]) + nt(lift_grad, w_up[...])
    pass_first(1)
    work = [
        (gate_out, hbm_gate_out, lambda: tn(full[0], gate_grad)),
        (lift_out, hbm_lift_out, lambda: tn(full[0], lift_grad)),
        (dexp_out, hbm_dexp_out, lambda: tn(hidden, full[1])),
    ]

    def do_work():
        held, out, product = work.pop(0)
        held[...] = product().astype(BF)
        copy = pltpu.make_async_copy(held, out, osem.at[len(work)])
        copy.start()
        pending.append(copy.wait)

    pass_second(0)
    do_work()
    pass_second(1)
    do_work()
    do_work()

    for p in range(2):
        back[p] = nn(unpack, pass_end(p)).astype(BF).reshape(ndp, PAD, LANE)
        for d in far(ndp):
            send(back.at[p, d], backr.at[p, d], 8 + p, dpeer(-d))
        backr[p, 0] = back[p, 0]

    for p in range(2):
        landed(backr.at[p, pl.ds(1, ndp - 1)], 8 + p)
        value = tn(pick[1 - p], backr[p].reshape(slots, LANE))
        z1[p] = value.astype(BF).reshape(nz, rows, LANE)
        for d in far(nz):
            send(z1.at[p, (z + d) % nz], z1r.at[p, d], 10 + p, zpeer(d))
    landed(z1r.at[0, pl.ds(1, nz - 1)], 10)
    cf1[z] = gathered(z1[0, z], z1r.at[0], nz).astype(BF)
    for d in far(nz):
        send(cf1.at[z], cf1.at[z], 12, zpeer(d))
    landed(z1r.at[1, pl.ds(1, nz - 1)], 11)
    cb1[:, mine] = gathered(z1[1, z], z1r.at[1], nz).astype(BF)
    for d in far(ny):
        send(cb1.at[:, mine], cb1.at[:, mine], 13, ypeer(d))
    landed(cf1.at[pl.ds(0, nz - 1)], 12)
    for d in far(ny):
        send(cf1, cf.at[:, :, mine], 14, ypeer(d))
    cf[:, :, mine] = cf1[...]
    landed(cb1.at[:, pl.ds(0, (ny - 1) * LANE)], 13)
    for d in far(nz):
        send(cb1, cb.at[z], 15, zpeer(d))
    cb[z] = cb1[...]

    share_rows = latent // ndp
    for p, (ref, wait) in enumerate((
        (cf, cf.at[:, :, pl.ds(0, (ny - 1) * LANE)]), (cb, cb.at[pl.ds(0, nz - 1)]),
    )):
        landed(wait, 14 + p)
        value = tn(ref[...].reshape(tok, latent), padded[p]).astype(BF)
        for q in range(ndp):
            g1[p, q % 2, q // 2] = value[q * share_rows:(q + 1) * share_rows]
        send(g1.at[p, 1 - core], g1r.at[p], 16 + p, sibling)
    for p in range(2):
        landed(g1r.at[p], 16 + p)
        g2[p] = (g1[p, core].astype(F32) + g1r[p].astype(F32)).astype(BF)
        for d in far(nx):
            send(g2.at[p, (xi + d) % nx], g2r.at[p, d], 18 + p, xpeer(d))
    layer_out[...] = nt(up[...], cf[...].reshape(tok, latent)).astype(BF)
    token_grad[...] = nt(down[...], cb[...].reshape(tok, latent)).astype(BF)
    for p, out in enumerate((up_grad, down_grad)):
        landed(g2r.at[p, pl.ds(1, nx - 1)], 18 + p)
        out[...] = gathered(g2[p, xi], g2r.at[p], nx)[:, :wide]
    finish()


def hand_over(count, *refs):
    given, outs, held = refs[:count], refs[count:2 * count], refs[2 * count:3 * count]
    arrived, left = refs[3 * count:]
    ins, out = [], []
    for n in range(count):
        rows = given[n].shape[0]
        step = min(rows, 128 * 1024 // given[n].shape[1])
        for at in range(0, rows, step):
            part, k = pl.ds(at, step), len(ins)
            ins.append(pltpu.make_async_copy(given[n].at[part], held[n].at[part], arrived.at[k]))
            out.append(pltpu.make_async_copy(held[n].at[part], outs[n].at[part], left.at[k]))
    for copy in ins:
        copy.start()
    for here, copy in zip(ins, out):
        here.wait()
        copy.start()
    for copy in out:
        copy.wait()


def make(mesh, ny):
    ndp, nex = mesh.shape["dp"], mesh.shape["expert"]
    nz = nex // ny
    nx = ndp // 2
    half = ny // 2

    def local(tokens, routes, scores, down, up, w_gate, w_up, w_down, cot):
        tokens, cot, up = tokens.T, cot.T, up.T
        wide, tok = tokens.shape
        latent, hid = w_gate.shape
        rows, part = tok // nz, latent // ndp
        packed = ndp * CAP
        shape = jax.ShapeDtypeStruct
        inside = pl.BlockSpec(memory_space=pltpu.VMEM)
        outside = pl.BlockSpec(memory_space=pl.ANY)

        def vm(*dims, kind=BF):
            return pltpu.VMEM(dims, kind)

        outs = pl.pallas_call(
            functools.partial(kernel, ndp, nz, ny),
            out_shape=(
                shape((wide, tok), BF),
                shape((wide, tok), BF),
                shape((part, wide), F32),
                shape((part, wide), F32),
                shape((latent, hid), BF),
                shape((latent, hid), BF),
                shape((hid, latent), BF),
            ),
            in_specs=[outside] + [inside] * 2 + [outside] * 6,
            out_specs=[inside] * 4 + [outside] * 3,
            scratch_shapes=[
                vm(wide, tok), vm(wide, latent), vm(wide, latent), vm(wide, tok),
                vm(latent, hid), vm(latent, hid), vm(hid, latent),
                vm(latent, hid), vm(latent, hid), vm(hid, latent),
                pltpu.SemaphoreType.DMA((7,)), pltpu.SemaphoreType.DMA((3,)),
                vm(ny, tok, LANE), vm(ny, tok, LANE), vm(nz, rows, LANE), vm(nz, rows, LANE),
                vm(nz, rows, latent), vm(nz, rows, latent), vm(ny, rows, LANE), vm(ny, rows, LANE),
                vm(2, nz, rows, LANE),
                vm(2, ndp * PAD, tok),
                vm(2, ndp, PAD, LANE), vm(2, ndp, PAD, LANE),
                vm(2, packed, latent),
                vm(2, half, 2 * CUT, packed // CUT, LANE), vm(2, half, 2 * CUT, packed // CUT, LANE),
                vm(2, packed, latent, kind=F32),
                vm(2, ndp, PAD, LANE), vm(2, ndp, PAD, LANE),
                vm(2, nz, rows, LANE), vm(2, nz, rows, LANE),
                vm(nz, rows, LANE), vm(rows, latent), vm(nz, rows, latent), vm(nz, rows, latent),
                vm(2, tok, LANE),
                vm(2, 2, nx, part, LANE), vm(2, nx, part, LANE), vm(2, nx, part, LANE), vm(2, nx, part, LANE),
                pltpu.SemaphoreType.DMA((20,)), pltpu.SemaphoreType.DMA((20,)),
                pltpu.SemaphoreType.DMA((2, half, 2 * CUT)), pltpu.SemaphoreType.DMA((2, half, 2 * CUT)),
                pltpu.SemaphoreType.DMA((2, half, 2 * CUT)), pltpu.SemaphoreType.DMA((2, half, 2 * CUT)),
            ],
            compiler_params=pltpu.CompilerParams(
                collective_id=0, has_side_effects=True, vmem_limit_bytes=56 * 1024 * 1024,
            ),
        )(tokens, routes.T, scores.T, down, up, w_gate, w_up, w_down, cot)
        layer_out, token_grad, down_grad, up_grad, gate_out, lift_out, dexp_out = pl.pallas_call(
            functools.partial(hand_over, len(outs)),
            out_shape=[shape(out.shape, out.dtype) for out in outs],
            in_specs=[outside] * len(outs),
            out_specs=[outside] * len(outs),
            scratch_shapes=[vm(*out.shape, kind=out.dtype) for out in outs] + [
                pltpu.SemaphoreType.DMA((16,)), pltpu.SemaphoreType.DMA((16,)),
            ],
            compiler_params=pltpu.CompilerParams(vmem_limit_bytes=58 * 1024 * 1024),
        )(*outs)
        return layer_out.T, token_grad.T, down_grad.T, up_grad, gate_out, lift_out, dexp_out

    return jax.shard_map(
        local, mesh=mesh,
        in_specs=(
            P("dp", "expert"), P("dp", None), P("dp", None), P("expert", None), P(None, "expert"),
            P(None, ("dp", "expert")), P(None, ("dp", "expert")), P(("dp", "expert"), None), P("dp", "expert"),
        ),
        out_specs=(
            P("dp", "expert"), P("dp", "expert"), P("expert", "dp"), P("dp", "expert"),
            P(None, ("dp", "expert")), P(None, ("dp", "expert")), P(("dp", "expert"), None),
        ),
        check_vma=False,
    )


def solution(mesh):
    return make(mesh, NY)
```

```python
import functools

import jax
import jax.numpy as jnp
from jax import lax
from jax.experimental import pallas as pl
from jax.experimental.pallas import tpu as pltpu
from jax.sharding import PartitionSpec as P

MESH = pl.DeviceIdType.MESH
BF = jnp.bfloat16
F32 = jnp.float32
NY = 8
CAP = 12
PAD = 16
LANE = 128
CUT = 1


def nn(a, b):
    return jnp.dot(a, b, preferred_element_type=F32)


def nt(a, b):
    return lax.dot_general(a, b, (((1,), (1,)), ((), ())), preferred_element_type=F32)


def tn(a, b):
    return lax.dot_general(a, b, (((0,), (0,)), ((), ())), preferred_element_type=F32)


def kernel(
    ndp, nz, ny,
    hbm_tokens, routes, scores, hbm_proj, hbm_back, hbm_gate, hbm_up, hbm_down, hbm_cot,
    layer_out, token_grad, down_grad, up_grad, hbm_gate_out, hbm_lift_out, hbm_dexp_out,
    tokens, down, up, cot, w_gate, w_up, w_down, gate_out, lift_out, dexp_out, isem, osem,
    f1, f1r, f2, f2r, b1, b1r, b2, b2r, low,
    pick, send4, recv4, full, ystage, yrecv, own, back, backr,
    z1, z1r, cf1, cb1, cf, cb, padded, g1, g1r, g2, g2r,
    ssem, rsem, ysend, yrcv, psend, prcv,
):
    dp = lax.axis_index("dp")
    ex = lax.axis_index("expert")
    z, y = ex // ny, ex % ny
    xi, core = dp // 2, dp % 2
    nx = ndp // 2
    wide, tok = tokens.shape
    latent = down.shape[1]
    rows = tok // nz
    slots = ndp * PAD
    packed = ndp * CAP

    def ypeer(d):
        return (dp, z * ny + (y + d + ny) % ny)

    def zpeer(d):
        return (dp, ((z + d + nz) % nz) * ny + y)

    def dpeer(d):
        return ((dp + d + ndp) % ndp, ex)

    def xpeer(d):
        return (((xi + d + nx) % nx) * 2 + core, ex)

    def far(count):
        return sorted(range(1, count), key=lambda d: -min(d, count - d))

    sibling = (xi * 2 + 1 - core, ex)

    pending = []

    def finish():
        for wait in pending:
            wait()

    fetch = [
        pltpu.make_async_copy(src, dst, isem.at[n])
        for n, (src, dst) in enumerate((
            (hbm_tokens, tokens), (hbm_proj, down), (hbm_cot, cot), (hbm_back, up),
            (hbm_gate, w_gate), (hbm_up, w_up), (hbm_down, w_down),
        ))
    ]
    for copy in fetch:
        copy.start()

    def send(src, dst, phase, device):
        pltpu.make_async_remote_copy(
            src_ref=src, dst_ref=dst, send_sem=ssem.at[phase], recv_sem=rsem.at[phase],
            device_id=device, device_id_type=MESH,
        ).start()

    def landed(ref, phase):
        whole = pltpu.make_async_remote_copy(
            src_ref=ref, dst_ref=ref, send_sem=ssem.at[phase], recv_sem=rsem.at[phase],
            device_id=sibling, device_id_type=MESH,
        )
        whole.wait_recv()
        pending.append(whole.wait_send)

    barrier = pltpu.get_barrier_semaphore()
    for d in range(1, ny):
        pl.semaphore_signal(barrier, inc=1, device_id=ypeer(d), device_id_type=MESH)
    for d in range(1, nz):
        pl.semaphore_signal(barrier, inc=1, device_id=zpeer(d), device_id_type=MESH)
    for d in range(1, ndp):
        pl.semaphore_signal(barrier, inc=1, device_id=dpeer(d), device_id_type=MESH)

    fetch[0].wait()
    fetch[1].wait()
    part = tn(tokens[...], down[...]).astype(BF)
    for q in range(ny):
        f1[q] = part[:, q * LANE:(q + 1) * LANE]
    pl.semaphore_wait(barrier, ny + nz + ndp - 3)
    for d in far(ny):
        send(f1.at[(y + d) % ny], f1r.at[d], 0, ypeer(d))
    fetch[2].wait()
    fetch[3].wait()
    part = tn(cot[...], up[...]).astype(BF)
    for q in range(nz):
        b1[q] = part[q * rows:(q + 1) * rows]
    for d in far(nz):
        send(b1.at[(z + d) % nz], b1r.at[d], 1, zpeer(d))

    r = routes[...]
    s = scores[...].astype(F32)
    share = s / jnp.sum(s, axis=0, keepdims=True)
    target = lax.broadcasted_iota(jnp.int32, (ndp, tok), 0) + dp
    target = jnp.where(target >= ndp, target - ndp, target) * nz + z
    member = jnp.zeros((ndp, tok), F32)
    weight = jnp.zeros((ndp, tok), F32)
    for k in range(r.shape[0]):
        hit = r[k:k + 1] == target
        member = member + jnp.where(hit, 1.0, 0.0)
        weight = weight + jnp.where(hit, share[k:k + 1], 0.0)
    ahead = lax.broadcasted_iota(jnp.int32, (tok, tok), 0) < lax.broadcasted_iota(jnp.int32, (tok, tok), 1)
    place = nn(member.astype(BF), jnp.where(ahead, 1.0, 0.0).astype(BF))
    place = jnp.where(member > 0.5, place, -1.0).astype(jnp.int32)
    spot = lax.broadcasted_iota(jnp.int32, (PAD, tok), 0)
    for d in range(ndp):
        hit = place[d:d + 1] == spot
        pick[0, d * PAD:(d + 1) * PAD] = jnp.where(hit, 1.0, 0.0).astype(BF)
        pick[1, d * PAD:(d + 1) * PAD] = jnp.where(hit, weight[d:d + 1], 0.0).astype(BF)
    row = lax.broadcasted_iota(jnp.int32, (packed, slots), 0)
    col = lax.broadcasted_iota(jnp.int32, (packed, slots), 1)
    pack = jnp.where((col - row == (col >> 4) * (PAD - CAP)) & ((col & (PAD - 1)) < CAP), 1.0, 0.0).astype(BF)
    row = lax.broadcasted_iota(jnp.int32, (slots, packed), 0)
    col = lax.broadcasted_iota(jnp.int32, (slots, packed), 1)
    unpack = jnp.where((row - col == (row >> 4) * (PAD - CAP)) & ((row & (PAD - 1)) < CAP), 1.0, 0.0).astype(BF)
    padded[...] = jnp.zeros_like(padded)
    padded[0, :, :wide] = cot[...].T
    padded[1, :, :wide] = tokens[...].T

    def gathered(first, others, count):
        total = first.astype(F32)
        for d in range(1, count):
            total = total + others[d].astype(F32)
        return total

    landed(f1r.at[pl.ds(1, ny - 1)], 0)
    total = gathered(f1[y], f1r, ny).astype(BF)
    for q in range(nz):
        f2[q] = total[q * rows:(q + 1) * rows]
    for d in far(nz):
        send(f2.at[(z + d) % nz], f2r.at[d], 2, zpeer(d))
    landed(b1r.at[pl.ds(1, nz - 1)], 1)
    total = gathered(b1[z], b1r, nz).astype(BF)
    for q in range(ny):
        b2[q] = total[:, q * LANE:(q + 1) * LANE]
    for d in far(ny):
        send(b2.at[(y + d) % ny], b2r.at[d], 3, ypeer(d))
    landed(f2r.at[pl.ds(1, nz - 1)], 2)
    low[0, z] = gathered(f2[z], f2r, nz).astype(BF)
    for d in far(nz):
        send(low.at[0, z], low.at[0, z], 4, zpeer(d))
    landed(b2r.at[pl.ds(1, ny - 1)], 3)
    low[1, z] = gathered(b2[y], b2r, ny).astype(BF)
    for d in far(nz):
        send(low.at[1, z], low.at[1, z], 5, zpeer(d))

    for p in range(2):
        landed(low.at[p, pl.ds(0, nz - 1)], 4 + p)
        value = nn(pick[p], low[p].reshape(tok, LANE))
        send4[p] = value.astype(BF).reshape(ndp, PAD, LANE)
        for d in far(ndp):
            send(send4.at[p, d], recv4.at[p, d], 6 + p, dpeer(d))
        recv4[p, 0] = send4[p, 0]

    mine = pl.ds(pl.multiple_of(y * LANE, LANE), LANE)
    piece = packed // CUT

    def lane(q):
        return pl.ds(pl.multiple_of(((q + ny) % ny) * LANE, LANE), LANE)

    def pieces(p):
        return [(k, way) for k in range(p * CUT, (p + 1) * CUT) for way in range(2)]

    def hop(way, leg, k):
        sign = 1 if way == 0 else -1
        source = y if leg < 2 else y - 2 * sign
        at = full.at[k // CUT, pl.ds(k % CUT * piece, piece), lane(source)]
        return pltpu.make_async_remote_copy(
            src_ref=at, dst_ref=at,
            send_sem=ysend.at[way, leg, k], recv_sem=yrcv.at[way, leg, k],
            device_id=ypeer(sign * (1 + leg % 2)), device_id_type=MESH,
        )

    def start(copy):
        copy.start()
        pending.append(copy.wait_send)

    for p in range(2):
        landed(recv4.at[p, pl.ds(1, ndp - 1)], 6 + p)
        full[p, :, mine] = nn(pack, recv4[p].reshape(slots, LANE)).astype(BF)
        for leg in ((1, 0), (1,))[p]:
            for k, way in pieces(p):
                start(hop(way, leg, k))
    for p in range(2):
        if p == 1:
            for k, way in pieces(p):
                start(hop(way, 0, k))
        for k, way in pieces(p):
            hop(way, 1, k).wait_recv()
            if way == k % 2:
                start(hop(way, 3, k))
            start(hop(way, 2, k))

    def gather_end(p):
        for k, way in pieces(p):
            hop(way, 0, k).wait_recv()
            hop(way, 2, k).wait_recv()
            if way == k % 2:
                hop(way, 3, k).wait_recv()

    gather_end(0)

    for copy in fetch[4:]:
        copy.wait()
    gate = nn(full[0], w_gate[...])
    lift = nn(full[0], w_up[...])
    sigma = jax.nn.sigmoid(gate)
    active = gate * sigma
    hidden = (active * lift).astype(BF)
    own[0] = nn(hidden, w_down[...])

    def block(p, k, to):
        return own[p, pl.ds(k % CUT * piece, piece), lane(to)]

    def pass_on(way, leg, k):
        sign = 1 if way == 0 else -1
        return pltpu.make_async_remote_copy(
            src_ref=ystage.at[way, leg, k], dst_ref=yrecv.at[way, leg, k],
            send_sem=psend.at[way, leg, k], recv_sem=prcv.at[way, leg, k],
            device_id=ypeer(sign * (1 + leg % 2)), device_id_type=MESH,
        )

    def pass_first(p):
        for k, way in pieces(p):
            sign = 1 if way == 0 else -1
            if way == k % 2:
                ystage[way, 3, k] = block(p, k, y + 4 * sign).astype(BF)
                start(pass_on(way, 3, k))
            ystage[way, 2, k] = block(p, k, y + 3 * sign).astype(BF)
            start(pass_on(way, 2, k))
        for k, way in pieces(p):
            sign = 1 if way == 0 else -1
            ystage[way, 0, k] = block(p, k, y + sign).astype(BF)
            start(pass_on(way, 0, k))

    def pass_second(p):
        for k, way in pieces(p):
            sign = 1 if way == 0 else -1
            value = block(p, k, y + 2 * sign)
            pass_on(way, 2, k).wait_recv()
            value = value + yrecv[way, 2, k].astype(F32)
            if way == k % 2:
                pass_on(way, 3, k).wait_recv()
                value = value + yrecv[way, 3, k].astype(F32)
            ystage[way, 1, k] = value.astype(BF)
            start(pass_on(way, 1, k))

    def pass_end(p):
        parts = []
        for k in range(p * CUT, (p + 1) * CUT):
            value = block(p, k, y)
            for way in range(2):
                for leg in (0, 1):
                    pass_on(way, leg, k).wait_recv()
                    value = value + yrecv[way, leg, k].astype(F32)
            parts.append(value.astype(BF))
        return jnp.concatenate(parts, axis=0)

    pass_first(0)
    gather_end(1)
    hidden_grad = nt(full[1], w_down[...])
    gate_grad = (hidden_grad * lift * (sigma * (1.0 + gate * (1.0 - sigma)))).astype(BF)
    lift_grad = (hidden_grad * active).astype(BF)
    own[1] = nt(gate_grad, w_gate[...]) + nt(lift_grad, w_up[...])
    pass_first(1)
    work = [
        (gate_out, hbm_gate_out, lambda: tn(full[0], gate_grad)),
        (lift_out, hbm_lift_out, lambda: tn(full[0], lift_grad)),
        (dexp_out, hbm_dexp_out, lambda: tn(hidden, full[1])),
    ]

    def do_work():
        held, out, product = work.pop(0)
        held[...] = product().astype(BF)
        copy = pltpu.make_async_copy(held, out, osem.at[len(work)])
        copy.start()
        pending.append(copy.wait)

    pass_second(0)
    do_work()
    pass_second(1)
    do_work()
    do_work()

    for p in range(2):
        back[p] = nn(unpack, pass_end(p)).astype(BF).reshape(ndp, PAD, LANE)
        for d in far(ndp):
            send(back.at[p, d], backr.at[p, d], 8 + p, dpeer(-d))
        backr[p, 0] = back[p, 0]

    for p in range(2):
        landed(backr.at[p, pl.ds(1, ndp - 1)], 8 + p)
        value = tn(pick[1 - p], backr[p].reshape(slots, LANE))
        z1[p] = value.astype(BF).reshape(nz, rows, LANE)
        for d in far(nz):
            send(z1.at[p, (z + d) % nz], z1r.at[p, d], 10 + p, zpeer(d))
    landed(z1r.at[0, pl.ds(1, nz - 1)], 10)
    cf1[z] = gathered(z1[0, z], z1r.at[0], nz).astype(BF)
    for d in far(nz):
        send(cf1.at[z], cf1.at[z], 12, zpeer(d))
    landed(z1r.at[1, pl.ds(1, nz - 1)], 11)
    cb1[:, mine] = gathered(z1[1, z], z1r.at[1], nz).astype(BF)
    for d in far(ny):
        send(cb1.at[:, mine], cb1.at[:, mine], 13, ypeer(d))
    landed(cf1.at[pl.ds(0, nz - 1)], 12)
    for d in far(ny):
        send(cf1, cf.at[:, :, mine], 14, ypeer(d))
    cf[:, :, mine] = cf1[...]
    landed(cb1.at[:, pl.ds(0, (ny - 1) * LANE)], 13)
    for d in far(nz):
        send(cb1, cb.at[z], 15, zpeer(d))
    cb[z] = cb1[...]

    share_rows = latent // ndp
    for p, (ref, wait) in enumerate((
        (cf, cf.at[:, :, pl.ds(0, (ny - 1) * LANE)]), (cb, cb.at[pl.ds(0, nz - 1)]),
    )):
        landed(wait, 14 + p)
        value = tn(ref[...].reshape(tok, latent), padded[p]).astype(BF)
        for q in range(ndp):
            g1[p, q % 2, q // 2] = value[q * share_rows:(q + 1) * share_rows]
        send(g1.at[p, 1 - core], g1r.at[p], 16 + p, sibling)
    for p in range(2):
        landed(g1r.at[p], 16 + p)
        g2[p] = (g1[p, core].astype(F32) + g1r[p].astype(F32)).astype(BF)
        for d in far(nx):
            send(g2.at[p, (xi + d) % nx], g2r.at[p, d], 18 + p, xpeer(d))
    layer_out[...] = nt(up[...], cf[...].reshape(tok, latent)).astype(BF)
    token_grad[...] = nt(down[...], cb[...].reshape(tok, latent)).astype(BF)
    for p, out in enumerate((up_grad, down_grad)):
        landed(g2r.at[p, pl.ds(1, nx - 1)], 18 + p)
        out[...] = gathered(g2[p, xi], g2r.at[p], nx)[:, :wide]
    finish()


def hand_over(count, *refs):
    given, outs, held = refs[:count], refs[count:2 * count], refs[2 * count:3 * count]
    arrived, left = refs[3 * count:]
    ins, out = [], []
    for n in range(count):
        rows = given[n].shape[0]
        step = min(rows, 128 * 1024 // given[n].shape[1])
        for at in range(0, rows, step):
            part, k = pl.ds(at, step), len(ins)
            ins.append(pltpu.make_async_copy(given[n].at[part], held[n].at[part], arrived.at[k]))
            out.append(pltpu.make_async_copy(held[n].at[part], outs[n].at[part], left.at[k]))
    for copy in ins:
        copy.start()
    for here, copy in zip(ins, out):
        here.wait()
        copy.start()
    for copy in out:
        copy.wait()


def make(mesh, ny):
    ndp, nex = mesh.shape["dp"], mesh.shape["expert"]
    nz = nex // ny
    nx = ndp // 2
    half = ny // 2

    def local(tokens, routes, scores, down, up, w_gate, w_up, w_down, cot):
        tokens, cot, up = tokens.T, cot.T, up.T
        wide, tok = tokens.shape
        latent, hid = w_gate.shape
        rows, part = tok // nz, latent // ndp
        packed = ndp * CAP
        shape = jax.ShapeDtypeStruct
        inside = pl.BlockSpec(memory_space=pltpu.VMEM)
        outside = pl.BlockSpec(memory_space=pl.ANY)

        def vm(*dims, kind=BF):
            return pltpu.VMEM(dims, kind)

        outs = pl.pallas_call(
            functools.partial(kernel, ndp, nz, ny),
            out_shape=(
                shape((wide, tok), BF),
                shape((wide, tok), BF),
                shape((part, wide), F32),
                shape((part, wide), F32),
                shape((latent, hid), BF),
                shape((latent, hid), BF),
                shape((hid, latent), BF),
            ),
            in_specs=[outside] + [inside] * 2 + [outside] * 6,
            out_specs=[inside] * 4 + [outside] * 3,
            scratch_shapes=[
                vm(wide, tok), vm(wide, latent), vm(wide, latent), vm(wide, tok),
                vm(latent, hid), vm(latent, hid), vm(hid, latent),
                vm(latent, hid), vm(latent, hid), vm(hid, latent),
                pltpu.SemaphoreType.DMA((7,)), pltpu.SemaphoreType.DMA((3,)),
                vm(ny, tok, LANE), vm(ny, tok, LANE), vm(nz, rows, LANE), vm(nz, rows, LANE),
                vm(nz, rows, latent), vm(nz, rows, latent), vm(ny, rows, LANE), vm(ny, rows, LANE),
                vm(2, nz, rows, LANE),
                vm(2, ndp * PAD, tok),
                vm(2, ndp, PAD, LANE), vm(2, ndp, PAD, LANE),
                vm(2, packed, latent),
                vm(2, half, 2 * CUT, packed // CUT, LANE), vm(2, half, 2 * CUT, packed // CUT, LANE),
                vm(2, packed, latent, kind=F32),
                vm(2, ndp, PAD, LANE), vm(2, ndp, PAD, LANE),
                vm(2, nz, rows, LANE), vm(2, nz, rows, LANE),
                vm(nz, rows, LANE), vm(rows, latent), vm(nz, rows, latent), vm(nz, rows, latent),
                vm(2, tok, LANE),
                vm(2, 2, nx, part, LANE), vm(2, nx, part, LANE), vm(2, nx, part, LANE), vm(2, nx, part, LANE),
                pltpu.SemaphoreType.DMA((20,)), pltpu.SemaphoreType.DMA((20,)),
                pltpu.SemaphoreType.DMA((2, half, 2 * CUT)), pltpu.SemaphoreType.DMA((2, half, 2 * CUT)),
                pltpu.SemaphoreType.DMA((2, half, 2 * CUT)), pltpu.SemaphoreType.DMA((2, half, 2 * CUT)),
            ],
            compiler_params=pltpu.CompilerParams(
                collective_id=0, has_side_effects=True, vmem_limit_bytes=56 * 1024 * 1024,
            ),
        )(tokens, routes.T, scores.T, down, up, w_gate, w_up, w_down, cot)
        layer_out, token_grad, down_grad, up_grad, gate_out, lift_out, dexp_out = pl.pallas_call(
            functools.partial(hand_over, len(outs)),
            out_shape=[shape(out.shape, out.dtype) for out in outs],
            in_specs=[outside] * len(outs),
            out_specs=[outside] * len(outs),
            scratch_shapes=[vm(*out.shape, kind=out.dtype) for out in outs] + [
                pltpu.SemaphoreType.DMA((16,)), pltpu.SemaphoreType.DMA((16,)),
            ],
            compiler_params=pltpu.CompilerParams(vmem_limit_bytes=58 * 1024 * 1024),
        )(*outs)
        return layer_out.T, token_grad.T, down_grad.T, up_grad, gate_out, lift_out, dexp_out

    return jax.shard_map(
        local, mesh=mesh,
        in_specs=(
            P("dp", "expert"), P("dp", None), P("dp", None), P("expert", None), P(None, "expert"),
            P(None, ("dp", "expert")), P(None, ("dp", "expert")), P(("dp", "expert"), None), P("dp", "expert"),
        ),
        out_specs=(
            P("dp", "expert"), P("dp", "expert"), P("expert", "dp"), P("dp", "expert"),
            P(None, ("dp", "expert")), P(None, ("dp", "expert")), P(("dp", "expert"), None),
        ),
        check_vma=False,
    )


def solution(mesh):
    return make(mesh, NY)
```
